32 devices in a mesh: row: 8 (over z, core), col: 4 (over y, x).
Axes of the slice: x: 2, y: 2, z: 4, core: 2. Of those that a mesh axis runs over, the one named last changes fastest.
Arguments:
- tokens: bfloat16 [2, 128, 128, 1024], P(None, 'row', 'col'), may hold values from -36 to 36
- norm_gain: float32 [1024], replicated, may hold values from 0.1 to 1.9
- w_query: bfloat16 [1024, 512], replicated, as said below
- w_kv: bfloat16 [1024, 1024], replicated, as said below
- w_out: bfloat16 [512, 1024], replicated, may hold values from -0.25 to 0.25
- w_pool: bfloat16 [4, 1024, 512], replicated, may hold values from -0.1875 to 0.1875
- w_join: bfloat16 [3, 3, 3072, 256], replicated, may hold values from -0.0390625 to 0.0390625
Outputs:
- joined: bfloat16 [2, 128, 128, 256], P(None, 'row', 'col')
The draws below stay inside these ranges and needn't reach their ends.
Inputs may be any that keep to these rules, and one draw needn't show every extreme that they name: `w_query`: entries within 6 / sqrt(1024) + 10 / 1024 of zero. `w_kv`: entries within 6 / sqrt(1024) + 10 / 1024 of zero.
All inputs are finite; a program needn't handle non-finite values.
Results may differ from the reference program's by a relative error of at most 0.003.
The reference program's roundings to bfloat16 on the way count: a program that leaves them out, or rounds other values in their place, can miss the bound.
Values may be sent and summed in bfloat16 or wider, within the bound.
A program may use at most 192 MiB of HBM per device.

```python
import math
import jax
import jax.numpy as jnp
from jax import lax

D = 1024
HEAD_DIM = 32
INNER = 512
BLOCK = 8
HALO = 2
PPM_CH = 512
CAT = 3072
JOIN_OUT = 256
SHEETS = 2
ROWS_DEV = 16
COLS_DEV = 32
GRID_H = 128
GRID_W = 128


def channel_normal(key):
    return jax.random.normal(jax.random.fold_in(key, 101), (D,), jnp.float32)


def draw_tokens(key, part):
    key_noise = jax.random.fold_in(key, 11)
    key_amplitude = jax.random.fold_in(key, 12)
    key_tile = jax.random.fold_in(key, 13)
    key_rowline = jax.random.fold_in(key, 14)
    key_colline = jax.random.fold_in(key, 15)
    key_rowstrength = jax.random.fold_in(key, 16)
    key_colstrength = jax.random.fold_in(key, 17)
    full_shape = (SHEETS, GRID_H, GRID_W, D)
    tiles_h = GRID_H // ROWS_DEV
    tiles_w = GRID_W // COLS_DEV
    channel_pattern = jnp.clip(channel_normal(key), -3.0, 3.0)
    token_noise = jnp.clip(jax.random.normal(key_noise, full_shape, jnp.float32), -4.0, 4.0)
    amplitude = jax.random.uniform(key_amplitude, (SHEETS, tiles_h, tiles_w), jnp.float32, 0.5, 1.5)
    tile_pattern = jnp.clip(jax.random.normal(key_tile, (SHEETS, tiles_h, tiles_w, D), jnp.float32), -2.5, 2.5)
    row_lines = jnp.clip(jax.random.normal(key_rowline, (SHEETS, GRID_H, D), jnp.float32), -2.0, 2.0)
    col_lines = jnp.clip(jax.random.normal(key_colline, (SHEETS, GRID_W, D), jnp.float32), -2.0, 2.0)
    row_strength = jax.random.uniform(key_rowstrength, (SHEETS, GRID_H, 1), jnp.float32, 2.0, 3.0)
    col_strength = jax.random.uniform(key_colstrength, (SHEETS, GRID_W, 1), jnp.float32, 2.0, 3.0)
    row_ramp = 1.0 + 2.0 * jnp.arange(tiles_h, dtype=jnp.float32) / max(tiles_h - 1, 1)
    amplitude = amplitude * row_ramp[None, :, None]
    amplitude = jnp.repeat(jnp.repeat(amplitude, ROWS_DEV, axis=1), COLS_DEV, axis=2)
    tile_part = jnp.repeat(jnp.repeat(tile_pattern, ROWS_DEV, axis=1), COLS_DEV, axis=2)
    line_part = (row_lines * row_strength)[:, :, None, :] + (col_lines * col_strength)[:, None, :, :]
    total = token_noise + amplitude[..., None] * channel_pattern + tile_part + line_part
    return total.astype(jnp.bfloat16)


def draw_w_query(key, part):
    random_part = jnp.clip(jax.random.normal(jax.random.fold_in(key, 202), (D, INNER), jnp.float32), -6.0, 6.0) * D ** (-0.5)
    return random_part.astype(jnp.bfloat16)


def draw_w_kv(key, part):
    random_part = jnp.clip(jax.random.normal(jax.random.fold_in(key, 303), (D, 2 * INNER), jnp.float32), -6.0, 6.0) * D ** (-0.5)
    return random_part.astype(jnp.bfloat16)


def normal_values(stream_key, shape, width, limit, kind=jnp.bfloat16):
    drawn = jax.random.normal(stream_key, shape, jnp.float32) * width
    return jnp.minimum(jnp.maximum(drawn, -limit), limit).astype(kind)


def setup_inputs(seed: int = 0) -> dict:
    arg_keys = jax.random.split(jax.random.key(seed), 8)
    tokens = draw_tokens(jax.random.fold_in(arg_keys[7], 71), 0)
    norm_gain = jnp.clip(1.0 + 0.18 * jax.random.normal(arg_keys[1], (D,), jnp.float32), 0.1, 1.9)
    w_query = draw_w_query(jax.random.fold_in(arg_keys[7], 71), 0)
    w_kv = draw_w_kv(jax.random.fold_in(arg_keys[7], 71), 0)
    w_out = normal_values(arg_keys[4], (INNER, D), INNER ** -0.5, 0.25)
    w_pool = normal_values(arg_keys[5], (4, D, PPM_CH), D ** -0.5, 0.1875)
    w_join = normal_values(arg_keys[6], (3, 3, CAT, JOIN_OUT), (9 * CAT) ** -0.5, 0.0390625)
    return dict(tokens=tokens, norm_gain=norm_gain, w_query=w_query, w_kv=w_kv, w_out=w_out, w_pool=w_pool, w_join=w_join)


EPS = 1e-05
pool_levels = (1, 2, 3, 6)

def unfold(extended, axis, count):
    pad_spec = [(0, 0)] * extended.ndim
    pad_spec[axis] = (0, BLOCK - 2 * HALO)
    extended = jnp.pad(extended, pad_spec)
    nblocks = count // BLOCK
    head_part = lax.slice_in_dim(extended, 0, count, axis=axis)
    tail_part = lax.slice_in_dim(extended, BLOCK, count + BLOCK, axis=axis)
    new_shape = extended.shape[:axis] + (nblocks, BLOCK) + extended.shape[axis + 1:]
    head_part = head_part.reshape(new_shape)
    tail_part = lax.slice_in_dim(tail_part.reshape(new_shape), 0, 2 * HALO, axis=axis + 1)
    return jnp.concatenate([head_part, tail_part], axis=axis + 1)

def attend(query_blocks, windows, row_ok, col_ok):
    sheets, nbr, _, nbc, _, inner = query_blocks.shape
    heads = inner // HEAD_DIM
    span = BLOCK + 2 * HALO
    queries = query_blocks.transpose(0, 1, 3, 2, 4, 5).reshape(sheets, nbr, nbc, BLOCK * BLOCK, heads, HEAD_DIM)
    window_kv = windows.transpose(0, 1, 3, 2, 4, 5).reshape(sheets, nbr, nbc, span * span, 2, heads, HEAD_DIM)
    keys = window_kv[:, :, :, :, 0]
    values = window_kv[:, :, :, :, 1]
    scores = jnp.einsum('sabqhe,sabkhe->sabhqk', queries.astype(jnp.float32), keys.astype(jnp.float32)) / math.sqrt(HEAD_DIM)
    allowed = row_ok[:, :, None, None] & col_ok[None, None, :, :]
    allowed = allowed.transpose(0, 2, 1, 3).reshape(nbr, nbc, 1, 1, span * span)
    scores = jnp.where(allowed[None], scores, -1e+30)
    top = lax.optimization_barrier(jnp.max(scores, axis=-1, keepdims=True))
    expon = jnp.exp(scores - top)
    weights = (expon / lax.optimization_barrier(jnp.sum(expon, axis=-1, keepdims=True))).astype(jnp.bfloat16)
    context = jnp.einsum('sabhqk,sabkhe->sabqhe', weights.astype(jnp.float32), values.astype(jnp.float32))
    context = context.astype(jnp.bfloat16).reshape(sheets, nbr, nbc, BLOCK, BLOCK, inner)
    return context.transpose(0, 1, 3, 2, 4, 5).reshape(sheets, nbr * BLOCK, nbc * BLOCK, inner)

def pool_matrix(level, length, first, count):
    places = first + jnp.arange(count)
    cells = jnp.arange(level)
    starts = cells * length // level
    ends = ((cells + 1) * length + level - 1) // level
    member = (places[None, :] >= starts[:, None]) & (places[None, :] < ends[:, None])
    return (member, ends - starts)

def upsample_matrix(level, length, first, count):
    places = first + jnp.arange(count)
    numer = jnp.maximum((2 * places + 1) * level - length, 0)
    lower = numer // (2 * length)
    frac = (numer - lower * 2 * length).astype(jnp.float32) / (2.0 * length)
    upper = jnp.minimum(lower + 1, level - 1)
    cells = jnp.arange(level)[None, :]
    weight = (cells == lower[:, None]) * (1.0 - frac)[:, None] + (cells == upper[:, None]) * frac[:, None]
    inside = ((places >= 0) & (places < length)).astype(jnp.float32)
    return weight * inside[:, None]

def reference(tokens, norm_gain, w_query, w_kv, w_out, w_pool, w_join):
    tokens_f = tokens.astype(jnp.float32)
    center = lax.optimization_barrier(jnp.mean(tokens_f, axis=-1, keepdims=True))
    spread = lax.optimization_barrier(jnp.mean((tokens_f - center) ** 2, axis=-1, keepdims=True))
    normed = ((tokens_f - center) * lax.rsqrt(spread + EPS) * norm_gain.astype(jnp.float32)).astype(jnp.bfloat16)
    queries = jnp.dot(normed, w_query, preferred_element_type=jnp.float32).astype(jnp.bfloat16)
    keyvals = jnp.dot(normed, w_kv, preferred_element_type=jnp.float32).astype(jnp.bfloat16)
    kv_padded = jnp.pad(keyvals, ((0, 0), (HALO, HALO), (HALO, HALO), (0, 0)))
    col_places = jnp.arange(GRID_W + 2 * HALO) - HALO
    col_ok = unfold((col_places >= 0) & (col_places < GRID_W), 0, GRID_W)

    def band_attend(band):
        query_band = lax.dynamic_slice_in_dim(queries, band * BLOCK, BLOCK, 1)
        query_blocks = query_band.reshape(SHEETS, 1, BLOCK, GRID_W // BLOCK, BLOCK, INNER)
        kv_band = lax.dynamic_slice_in_dim(kv_padded, band * BLOCK, BLOCK + 2 * HALO, 1)
        kv_band = kv_band.reshape(SHEETS, 1, BLOCK + 2 * HALO, GRID_W + 2 * HALO, 2 * INNER)
        windows = unfold(kv_band, 3, GRID_W)
        row_places = band * BLOCK - HALO + jnp.arange(BLOCK + 2 * HALO)
        row_ok = ((row_places >= 0) & (row_places < GRID_H))[None, :]
        return attend(query_blocks, windows, row_ok, col_ok)[:, 0:BLOCK]
    context = lax.map(band_attend, jnp.arange(GRID_H // BLOCK))
    context = context.transpose(1, 0, 2, 3, 4).reshape(SHEETS, GRID_H, GRID_W, INNER)
    attended = (tokens_f + jnp.dot(context, w_out, preferred_element_type=jnp.float32)).astype(jnp.bfloat16)
    branches = []
    for index, level in enumerate(pool_levels):
        rows_in, rows_count = pool_matrix(level, GRID_H, 0, GRID_H)
        cols_in, cols_count = pool_matrix(level, GRID_W, 0, GRID_W)
        row_sums = jnp.einsum('ir,srcd->sicd', rows_in.astype(attended.dtype), attended, preferred_element_type=jnp.float32)
        sums = jnp.einsum('jc,sicd->sijd', cols_in.astype(jnp.float32), row_sums, precision=lax.Precision.HIGHEST)
        counts = (rows_count[:, None] * cols_count[None, :]).astype(jnp.float32)
        pooled = sums / counts[None, :, :, None]
        branch = jnp.einsum('sijd,dp->sijp', pooled, w_pool[index].astype(jnp.float32), precision=lax.Precision.HIGHEST)
        branches.append(jnp.maximum(branch, 0.0))
    att_padded = jnp.pad(attended, ((0, 0), (1, 1), (1, 1), (0, 0)))
    col_maps = [upsample_matrix(level, GRID_W, -1, GRID_W + 2) for level in pool_levels]

    def join_band(band):
        first = band * ROWS_DEV
        pieces = [lax.dynamic_slice_in_dim(att_padded, first, ROWS_DEV + 2, 1)]
        for index, level in enumerate(pool_levels):
            row_map = upsample_matrix(level, GRID_H, first - 1, ROWS_DEV + 2)
            grown = jnp.einsum('ri,sijc,wj->srwc', row_map, branches[index], col_maps[index], precision=lax.Precision.HIGHEST)
            pieces.append(grown.astype(jnp.bfloat16))
        stacked = jnp.concatenate(pieces, axis=-1)
        total = jnp.zeros((SHEETS, ROWS_DEV, GRID_W, JOIN_OUT), jnp.float32)
        for shift_row in range(3):
            for shift_col in range(3):
                total = total + jnp.dot(stacked[:, shift_row:shift_row + ROWS_DEV, shift_col:shift_col + GRID_W], w_join[shift_row, shift_col], preferred_element_type=jnp.float32)
        return total.astype(jnp.bfloat16)
    joined = lax.map(join_band, jnp.arange(GRID_H // ROWS_DEV))
    return joined.transpose(1, 0, 2, 3, 4).reshape(SHEETS, GRID_H, GRID_W, JOIN_OUT)
```

```python
import functools
import math

import jax
import jax.numpy as jnp
from jax import lax
from jax.experimental import pallas as pl
from jax.experimental.pallas import tpu as pltpu
from jax.sharding import PartitionSpec as P

HEAD_DIM = 32
BLOCK = 8
HALO = 2
SPAN = BLOCK + 2 * HALO
WIDE = 16
LANES = 256
BINS = 64
MESH = pl.DeviceIdType.MESH

EPS = 1e-05
pool_levels = (1, 2, 3, 6)


def padded(cells, sides, width):
    for axis, dim in sides:
        count = lax.axis_size(axis)
        ends = count - 1
        head = lax.slice_in_dim(cells, 0, width, axis=dim)
        tail = lax.slice_in_dim(cells, cells.shape[dim] - width, cells.shape[dim], axis=dim)
        cells = jnp.concatenate(
            [
                lax.ppermute(tail, axis, [(i, (i + 1) % count) for i in range(ends)]),
                cells,
                lax.ppermute(head, axis, [((i + 1) % count, i) for i in range(ends)]),
            ],
            axis=dim,
        )
    return cells


def pool_matrix(level, length, first, count):
    places = first + jnp.arange(count)
    cells = jnp.arange(level)
    starts = cells * length // level
    ends = ((cells + 1) * length + level - 1) // level
    member = (places[None, :] >= starts[:, None]) & (places[None, :] < ends[:, None])
    return (member, ends - starts)


def upsample_matrix(level, length, first, count):
    places = first + jnp.arange(count)
    numer = jnp.maximum((2 * places + 1) * level - length, 0)
    lower = numer // (2 * length)
    frac = (numer - lower * 2 * length).astype(jnp.float32) / (2.0 * length)
    upper = jnp.minimum(lower + 1, level - 1)
    cells = jnp.arange(level)[None, :]
    weight = (cells == lower[:, None]) * (1.0 - frac)[:, None] + (cells == upper[:, None]) * frac[
        :, None
    ]
    inside = ((places >= 0) & (places < length)).astype(jnp.float32)
    return weight * inside[:, None]


def attend_kernel(pos, q_ref, kv_ref, tok_ref, wout_ref, pool_ref, att_ref, part_ref, ctx):
    band = pl.program_id(1)
    cols = q_ref.shape[2]
    inner = q_ref.shape[3]
    keys = SPAN * WIDE
    group = LANES // HEAD_DIM
    quers = BLOCK * BLOCK
    factor = math.log2(math.e) / math.sqrt(HEAD_DIM)
    place = lax.broadcasted_iota(jnp.int32, (keys, group * quers), 0)
    k_row = place // WIDE
    k_col = place % WIDE
    g_row = pos[0] + band * BLOCK - HALO + k_row
    row_ok = (g_row >= 0) & (g_row < pos[1]) & (k_col < SPAN)
    q_head = lax.broadcasted_iota(jnp.int32, (quers, LANES), 1) // HEAD_DIM
    rows = pl.ds(band * BLOCK, SPAN)
    for b in range(cols // BLOCK):
        g_col = pos[2] + b * BLOCK - HALO + k_col
        allowed = row_ok & (g_col >= 0) & (g_col < pos[3])
        for g in range(inner // LANES):
            lanes = slice(g * LANES, (g + 1) * LANES)
            vlanes = slice(inner + g * LANES, inner + (g + 1) * LANES)
            q = q_ref[0, :, b * BLOCK : (b + 1) * BLOCK, lanes].reshape(quers, LANES)
            wcols = slice(b * BLOCK, b * BLOCK + WIDE)
            k = kv_ref[0, rows, wcols, lanes].reshape(keys, LANES).astype(jnp.bfloat16)
            v = kv_ref[0, rows, wcols, vlanes].reshape(keys, LANES).astype(jnp.bfloat16)
            stack = jnp.concatenate(
                [jnp.where(q_head == h, q, 0.0) for h in range(group)], axis=0
            ).astype(jnp.bfloat16)
            scores = lax.dot_general(
                k, stack, (((1,), (1,)), ((), ())), preferred_element_type=jnp.float32
            )
            scores = jnp.where(allowed, scores, -1e30)
            top = jnp.max(scores, axis=0, keepdims=True)
            expon = jnp.exp2((scores - top) * factor)
            total = jnp.sum(expon, axis=0, keepdims=True)
            probs = (expon * (1.0 / total)).astype(jnp.bfloat16)
            out = lax.dot_general(
                v, probs, (((0,), (0,)), ((), ())), preferred_element_type=jnp.float32
            )
            pairs = jnp.concatenate(
                [
                    out[h * HEAD_DIM : (h + 1) * HEAD_DIM, (h // 2) * 2 * quers : (h // 2 + 1) * 2 * quers]
                    for h in range(group)
                ],
                axis=0,
            )
            turned = pairs.T
            got = jnp.where(q_head % 2 == 0, turned[:quers], turned[quers:])
            ctx[:, b * BLOCK : (b + 1) * BLOCK, lanes] = got.reshape(BLOCK, BLOCK, LANES)
    flat = ctx[...].reshape(BLOCK * cols, inner).astype(jnp.bfloat16)
    mixed = jnp.dot(flat, wout_ref[...], preferred_element_type=jnp.float32)
    tok = tok_ref[0].reshape(BLOCK * cols, -1).astype(jnp.float32)
    att = (tok + mixed).astype(jnp.bfloat16)
    att_ref[0] = att.reshape(BLOCK, cols, -1)
    part = jnp.dot(pool_ref[0], att, preferred_element_type=jnp.float32)

    @pl.when(band == 0)
    def _():
        part_ref[0] = part

    @pl.when(band != 0)
    def _():
        part_ref[0] = part_ref[0] + part


def attend(pos, queries, kv, tokens, w_out, pool):
    sheets, rows, cols, inner = queries.shape
    width = tokens.shape[-1]
    bands = rows // BLOCK
    return pl.pallas_call(
        attend_kernel,
        grid=(sheets, bands),
        in_specs=[
            pl.BlockSpec(memory_space=pltpu.SMEM),
            pl.BlockSpec((1, BLOCK, cols, inner), lambda s, a: (s, a, 0, 0)),
            pl.BlockSpec((1,) + kv.shape[1:], lambda s, a: (s, 0, 0, 0)),
            pl.BlockSpec((1, BLOCK, cols, width), lambda s, a: (s, a, 0, 0)),
            pl.BlockSpec(w_out.shape, lambda s, a: (0, 0)),
            pl.BlockSpec((1,) + pool.shape[1:], lambda s, a: (a, 0, 0)),
        ],
        out_specs=[
            pl.BlockSpec((1, BLOCK, cols, width), lambda s, a: (s, a, 0, 0)),
            pl.BlockSpec((1, BINS, width), lambda s, a: (s, 0, 0)),
        ],
        out_shape=[
            jax.ShapeDtypeStruct((sheets, rows, cols, width), jnp.bfloat16),
            jax.ShapeDtypeStruct((sheets, BINS, width), jnp.float32),
        ],
        scratch_shapes=[pltpu.VMEM((BLOCK, cols, inner), jnp.float32)],
        compiler_params=pltpu.CompilerParams(vmem_limit_bytes=40 * 2**20),
        name="attend",
    )(pos, queries, kv, tokens, w_out, pool)


def reduce_kernel(n_row, n_col, x_ref, o_ref, land, acc, side, s1, r1, s2, r2, s3, r3):
    row = lax.axis_index("row")
    col = lax.axis_index("col")
    size = acc.shape[0]
    barrier = pltpu.get_barrier_semaphore()
    peers = []
    for d in range(1, n_row):
        peers.append((lax.rem(row + d, n_row), col))
    for d in range(1, n_col):
        peers.append((row, lax.rem(col + d, n_col)))
    for peer in peers:
        pl.semaphore_signal(barrier, inc=1, device_id=peer, device_id_type=MESH)
    pl.semaphore_wait(barrier, len(peers))

    def part(index):
        return pl.ds(pl.multiple_of(index * size, size), size)

    mine = part(row)
    first = []
    for d in range(1, n_row):
        to = lax.rem(row + d, n_row)
        copy = pltpu.make_async_remote_copy(
            src_ref=x_ref.at[part(to)],
            dst_ref=land.at[d - 1],
            send_sem=s1.at[d - 1],
            recv_sem=r1.at[d - 1],
            device_id=(to, col),
            device_id_type=MESH,
        )
        copy.start()
        first.append(copy)
    total = x_ref[mine]
    for d in range(1, n_row):
        first[d - 1].wait_recv()
        total = total + land[d - 1]
    acc[...] = total
    second = []
    for d in range(1, n_col):
        copy = pltpu.make_async_remote_copy(
            src_ref=acc,
            dst_ref=side.at[d - 1],
            send_sem=s2.at[d - 1],
            recv_sem=r2.at[d - 1],
            device_id=(row, lax.rem(col + d, n_col)),
            device_id_type=MESH,
        )
        copy.start()
        second.append(copy)
    for d in range(1, n_col):
        second[d - 1].wait_recv()
        total = total + side[d - 1]
    o_ref[mine] = total
    third = []
    for d in range(1, n_row):
        copy = pltpu.make_async_remote_copy(
            src_ref=o_ref.at[mine],
            dst_ref=o_ref.at[mine],
            send_sem=s3.at[d - 1],
            recv_sem=r3.at[d - 1],
            device_id=(lax.rem(row + d, n_row), col),
            device_id_type=MESH,
        )
        copy.start()
        third.append(copy)
    for copy in third:
        copy.wait_recv()
    for copy in first + second + third:
        copy.wait_send()


def reduce_all(x):
    n_row = lax.axis_size("row")
    n_col = lax.axis_size("col")
    rows, width = x.shape
    size = rows // n_row
    dma = pltpu.SemaphoreType.DMA
    return pl.pallas_call(
        functools.partial(reduce_kernel, n_row, n_col),
        out_shape=jax.ShapeDtypeStruct(x.shape, x.dtype),
        in_specs=[pl.BlockSpec(memory_space=pltpu.VMEM)],
        out_specs=pl.BlockSpec(memory_space=pltpu.VMEM),
        scratch_shapes=[
            pltpu.VMEM((n_row - 1, size, width), jnp.float32),
            pltpu.VMEM((size, width), jnp.float32),
            pltpu.VMEM((n_col - 1, size, width), jnp.float32),
            dma((n_row - 1,)),
            dma((n_row - 1,)),
            dma((n_col - 1,)),
            dma((n_col - 1,)),
            dma((n_row - 1,)),
            dma((n_row - 1,)),
        ],
        compiler_params=pltpu.CompilerParams(
            collective_id=0, has_side_effects=True, vmem_limit_bytes=16 * 2**20
        ),
        cost_estimate=pl.CostEstimate(flops=10**6, bytes_accessed=6 * 10**7, transcendentals=0),
        name="reduce_all",
    )(x)


def split(x):
    high = x.astype(jnp.bfloat16)
    low = (x - high.astype(jnp.float32)).astype(jnp.bfloat16)
    return high, low


def join_kernel(sum_ref, count_ref, wpool_ref, att_ref, w_ref, up_ref, out_ref, branch, acc):
    step = pl.program_id(0) * 3 + pl.program_id(1)
    sheets, _, cols, width = att_ref.shape[1:]
    rows = out_ref.shape[1]
    ppm = wpool_ref.shape[2]
    total = sheets * BINS

    @pl.when(step == 0)
    def _():
        pooled = jnp.concatenate(split(sum_ref[...] / count_ref[...]), axis=0)
        slot = lax.broadcasted_iota(jnp.int32, (total, ppm), 0) % BINS
        start = 0
        for index, level in enumerate(pool_levels):
            here = (slot >= start) & (slot < start + level * level)
            start += level * level
            both = jnp.dot(pooled, wpool_ref[index], preferred_element_type=jnp.float32)
            grown = jnp.where(here, jnp.maximum(both[:total] + both[total:], 0.0), 0.0)
            high, low = split(grown)
            if level == 1:
                low = jnp.zeros_like(low)
            branch[:total, index * ppm : (index + 1) * ppm] = high
            branch[total:, index * ppm : (index + 1) * ppm] = low

    shift = pl.program_id(1)
    both = jnp.dot(branch[...], w_ref[0, 0, width:], preferred_element_type=jnp.float32)
    high, low = split(both[:total] + both[total:])
    for s in range(sheets):
        part = slice(s * BINS, (s + 1) * BINS)
        bins = jnp.concatenate([high[part], high[part], low[part]], axis=0)
        cells = att_ref[0, s, pl.ds(shift, rows)].reshape(rows * cols, width)
        term = jnp.dot(cells, w_ref[0, 0, :width], preferred_element_type=jnp.float32)
        term = term + jnp.dot(up_ref[0], bins, preferred_element_type=jnp.float32)

        @pl.when(step == 0)
        def _():
            acc[s] = term

        @pl.when(step != 0)
        def _():
            acc[s] = acc[s] + term

        @pl.when(step == 8)
        def _():
            out_ref[s] = acc[s].astype(jnp.bfloat16).reshape(rows, cols, -1)


def join(sums, counts, w_pool, shifted, w_join, ups):
    _, sheets, rows2, cols, width = shifted.shape
    rows = rows2 - 2
    cat, outs = w_join.shape[2:]
    ppm = w_pool.shape[2]
    return pl.pallas_call(
        join_kernel,
        grid=(3, 3),
        in_specs=[
            pl.BlockSpec(sums.shape, lambda c, a: (0, 0)),
            pl.BlockSpec(counts.shape, lambda c, a: (0, 0)),
            pl.BlockSpec(w_pool.shape, lambda c, a: (0, 0, 0)),
            pl.BlockSpec((1,) + shifted.shape[1:], lambda c, a: (c, 0, 0, 0, 0)),
            pl.BlockSpec((1, 1, cat, outs), lambda c, a: (a, c, 0, 0)),
            pl.BlockSpec((1,) + ups.shape[1:], lambda c, a: (a * 3 + c, 0, 0)),
        ],
        out_specs=pl.BlockSpec((sheets, rows, cols, outs), lambda c, a: (0, 0, 0, 0)),
        out_shape=jax.ShapeDtypeStruct((sheets, rows, cols, outs), jnp.bfloat16),
        scratch_shapes=[
            pltpu.VMEM((2 * sheets * BINS, 4 * ppm), jnp.bfloat16),
            pltpu.VMEM((sheets, rows * cols, outs), jnp.float32),
        ],
        compiler_params=pltpu.CompilerParams(vmem_limit_bytes=48 * 2**20),
        name="join",
    )(sums, counts, w_pool, shifted, w_join, ups)


def body(tokens, norm_gain, w_query, w_kv, w_out, w_pool, w_join):
    sheets, rows_here, cols_here, width = tokens.shape
    row_index = lax.axis_index("row")
    col_index = lax.axis_index("col")
    grid_h = rows_here * lax.axis_size("row")
    grid_w = cols_here * lax.axis_size("col")
    row_first = row_index * rows_here
    col_first = col_index * cols_here
    tokens_f = tokens.astype(jnp.float32)
    center = jnp.mean(tokens_f, axis=-1, keepdims=True)
    spread = jnp.mean((tokens_f - center) ** 2, axis=-1, keepdims=True)
    normed = ((tokens_f - center) * lax.rsqrt(spread + EPS) * norm_gain).astype(jnp.bfloat16)
    queries = jnp.dot(normed, w_query, preferred_element_type=jnp.float32)
    keyvals = jnp.dot(normed, w_kv, preferred_element_type=jnp.float32).astype(jnp.bfloat16)
    kv = padded(keyvals, (("row", 1), ("col", 2)), HALO).astype(jnp.float32)
    kv = jnp.pad(kv, ((0, 0), (0, 0), (0, WIDE - SPAN), (0, 0)))

    pools, counts, ups = [], [], []
    row_maps, col_maps = [], []
    for level in pool_levels:
        rows_in, rows_count = pool_matrix(level, grid_h, row_first, rows_here)
        cols_in, cols_count = pool_matrix(level, grid_w, col_first, cols_here)
        member = rows_in[:, None, :, None] & cols_in[None, :, None, :]
        pools.append(member.reshape(level * level, rows_here * cols_here))
        counts.append((rows_count[:, None] * cols_count[None, :]).reshape(-1))
        row_maps.append(upsample_matrix(level, grid_h, row_first - 1, rows_here + 2))
        col_maps.append(upsample_matrix(level, grid_w, col_first - 1, cols_here + 2))
    used = sum(level * level for level in pool_levels)
    pool = jnp.pad(jnp.concatenate(pools), ((0, BINS - used), (0, 0))).astype(jnp.bfloat16)
    bands = rows_here // BLOCK
    pool = pool.reshape(BINS, bands, BLOCK * cols_here).transpose(1, 0, 2)
    counts = jnp.pad(jnp.concatenate(counts), (0, BINS - used), constant_values=1)
    counts = jnp.tile(counts.astype(jnp.float32), sheets)[:, None]
    row_all = jnp.concatenate([jnp.repeat(m, l, axis=1) for m, l in zip(row_maps, pool_levels)], 1)
    col_all = jnp.concatenate([jnp.tile(m, (1, l)) for m, l in zip(col_maps, pool_levels)], 1)
    row_all = jnp.pad(row_all, ((0, 0), (0, BINS - used)))
    col_all = jnp.pad(col_all, ((0, 0), (0, BINS - used)))
    row_taps = jnp.stack([row_all[a : a + rows_here] for a in range(3)])
    col_taps = jnp.stack([col_all[c : c + cols_here] for c in range(3)])
    up = row_taps[:, None, :, None, :] * col_taps[None, :, None, :, :]
    up = up.reshape(9, rows_here * cols_here, BINS)
    up_high = lax.reduce_precision(up, 8, 7)
    up_low = (up - up_high).astype(jnp.bfloat16)
    up_high = up_high.astype(jnp.bfloat16)
    ups = jnp.concatenate([up_high, up_low, up_high], axis=-1)

    pos = jnp.stack([row_first, jnp.int32(grid_h), col_first, jnp.int32(grid_w)]).astype(jnp.int32)
    attended, partial = attend(pos, queries, kv, tokens, w_out, pool)
    sums = reduce_all(partial.reshape(sheets * BINS, width))
    extended = padded(attended, (("row", 1), ("col", 2)), 1)
    shifted = jnp.stack([extended[:, :, c : c + cols_here] for c in range(3)])
    return join(sums, counts, w_pool, shifted, w_join, ups)


def solution(mesh):
    placed = (P(None, "row", "col", None), P(), P(), P(), P(), P(), P())
    return jax.shard_map(
        body, mesh=mesh, in_specs=placed, out_specs=P(None, "row", "col", None), check_vma=False
    )
```

```python
import functools
import math

import jax
import jax.numpy as jnp
from jax import lax
from jax.experimental import pallas as pl
from jax.experimental.pallas import tpu as pltpu
from jax.sharding import PartitionSpec as P

HEAD_DIM = 32
BLOCK = 8
HALO = 2
SPAN = BLOCK + 2 * HALO
WIDE = 16
LANES = 256
BINS = 64
MESH = pl.DeviceIdType.MESH

EPS = 1e-05
pool_levels = (1, 2, 3, 6)


def padded(cells, sides, width):
    for axis, dim in sides:
        count = lax.axis_size(axis)
        ends = count - 1
        head = lax.slice_in_dim(cells, 0, width, axis=dim)
        tail = lax.slice_in_dim(cells, cells.shape[dim] - width, cells.shape[dim], axis=dim)
        cells = jnp.concatenate(
            [
                lax.ppermute(tail, axis, [(i, (i + 1) % count) for i in range(ends)]),
                cells,
                lax.ppermute(head, axis, [((i + 1) % count, i) for i in range(ends)]),
            ],
            axis=dim,
        )
    return cells


def pool_matrix(level, length, first, count):
    places = first + jnp.arange(count)
    cells = jnp.arange(level)
    starts = cells * length // level
    ends = ((cells + 1) * length + level - 1) // level
    member = (places[None, :] >= starts[:, None]) & (places[None, :] < ends[:, None])
    return (member, ends - starts)


def upsample_matrix(level, length, first, count):
    places = first + jnp.arange(count)
    numer = jnp.maximum((2 * places + 1) * level - length, 0)
    lower = numer // (2 * length)
    frac = (numer - lower * 2 * length).astype(jnp.float32) / (2.0 * length)
    upper = jnp.minimum(lower + 1, level - 1)
    cells = jnp.arange(level)[None, :]
    weight = (cells == lower[:, None]) * (1.0 - frac)[:, None] + (cells == upper[:, None]) * frac[
        :, None
    ]
    inside = ((places >= 0) & (places < length)).astype(jnp.float32)
    return weight * inside[:, None]


def attend_kernel(pos, q_ref, kv_ref, tok_ref, wout_ref, pool_ref, att_ref, part_ref, ctx):
    band = pl.program_id(1)
    cols = q_ref.shape[2]
    inner = q_ref.shape[3]
    keys = SPAN * WIDE
    group = LANES // HEAD_DIM
    quers = BLOCK * BLOCK
    factor = math.log2(math.e) / math.sqrt(HEAD_DIM)
    place = lax.broadcasted_iota(jnp.int32, (keys, group * quers), 0)
    k_row = place // WIDE
    k_col = place % WIDE
    g_row = pos[0] + band * BLOCK - HALO + k_row
    row_ok = (g_row >= 0) & (g_row < pos[1]) & (k_col < SPAN)
    q_head = lax.broadcasted_iota(jnp.int32, (quers, LANES), 1) // HEAD_DIM
    rows = pl.ds(band * BLOCK, SPAN)
    for b in range(cols // BLOCK):
        g_col = pos[2] + b * BLOCK - HALO + k_col
        allowed = row_ok & (g_col >= 0) & (g_col < pos[3])
        for g in range(inner // LANES):
            lanes = slice(g * LANES, (g + 1) * LANES)
            vlanes = slice(inner + g * LANES, inner + (g + 1) * LANES)
            q = q_ref[0, :, b * BLOCK : (b + 1) * BLOCK, lanes].reshape(quers, LANES)
            wcols = slice(b * BLOCK, b * BLOCK + WIDE)
            k = kv_ref[0, rows, wcols, lanes].reshape(keys, LANES).astype(jnp.bfloat16)
            v = kv_ref[0, rows, wcols, vlanes].reshape(keys, LANES).astype(jnp.bfloat16)
            stack = jnp.concatenate(
                [jnp.where(q_head == h, q, 0.0) for h in range(group)], axis=0
            ).astype(jnp.bfloat16)
            scores = lax.dot_general(
                k, stack, (((1,), (1,)), ((), ())), preferred_element_type=jnp.float32
            )
            scores = jnp.where(allowed, scores, -1e30)
            top = jnp.max(scores, axis=0, keepdims=True)
            expon = jnp.exp2((scores - top) * factor)
            total = jnp.sum(expon, axis=0, keepdims=True)
            probs = (expon * (1.0 / total)).astype(jnp.bfloat16)
            out = lax.dot_general(
                v, probs, (((0,), (0,)), ((), ())), preferred_element_type=jnp.float32
            )
            pairs = jnp.concatenate(
                [
                    out[h * HEAD_DIM : (h + 1) * HEAD_DIM, (h // 2) * 2 * quers : (h // 2 + 1) * 2 * quers]
                    for h in range(group)
                ],
                axis=0,
            )
            turned = pairs.T
            got = jnp.where(q_head % 2 == 0, turned[:quers], turned[quers:])
            ctx[:, b * BLOCK : (b + 1) * BLOCK, lanes] = got.reshape(BLOCK, BLOCK, LANES)
    flat = ctx[...].reshape(BLOCK * cols, inner).astype(jnp.bfloat16)
    mixed = jnp.dot(flat, wout_ref[...], preferred_element_type=jnp.float32)
    tok = tok_ref[0].reshape(BLOCK * cols, -1).astype(jnp.float32)
    att = (tok + mixed).astype(jnp.bfloat16)
    att_ref[0] = att.reshape(BLOCK, cols, -1)
    part = jnp.dot(pool_ref[0], att, preferred_element_type=jnp.float32)

    @pl.when(band == 0)
    def _():
        part_ref[0] = part

    @pl.when(band != 0)
    def _():
        part_ref[0] = part_ref[0] + part


def attend(pos, queries, kv, tokens, w_out, pool):
    sheets, rows, cols, inner = queries.shape
    width = tokens.shape[-1]
    bands = rows // BLOCK
    return pl.pallas_call(
        attend_kernel,
        grid=(sheets, bands),
        in_specs=[
            pl.BlockSpec(memory_space=pltpu.SMEM),
            pl.BlockSpec((1, BLOCK, cols, inner), lambda s, a: (s, a, 0, 0)),
            pl.BlockSpec((1,) + kv.shape[1:], lambda s, a: (s, 0, 0, 0)),
            pl.BlockSpec((1, BLOCK, cols, width), lambda s, a: (s, a, 0, 0)),
            pl.BlockSpec(w_out.shape, lambda s, a: (0, 0)),
            pl.BlockSpec((1,) + pool.shape[1:], lambda s, a: (a, 0, 0)),
        ],
        out_specs=[
            pl.BlockSpec((1, BLOCK, cols, width), lambda s, a: (s, a, 0, 0)),
            pl.BlockSpec((1, BINS, width), lambda s, a: (s, 0, 0)),
        ],
        out_shape=[
            jax.ShapeDtypeStruct((sheets, rows, cols, width), jnp.bfloat16),
            jax.ShapeDtypeStruct((sheets, BINS, width), jnp.float32),
        ],
        scratch_shapes=[pltpu.VMEM((BLOCK, cols, inner), jnp.float32)],
        compiler_params=pltpu.CompilerParams(vmem_limit_bytes=40 * 2**20),
        name="attend",
    )(pos, queries, kv, tokens, w_out, pool)


def reduce_kernel(n_row, n_col, x_ref, o_ref, xs, ys, land, acc, side, s1, r1, s2, r2, s3, r3, s4, r4):
    row = lax.axis_index("row")
    col = lax.axis_index("col")
    large = acc.shape[0]
    small = side.shape[1]
    lanes = xs.shape[2]
    barrier = pltpu.get_barrier_semaphore()
    by_row = [(lax.rem(row + d, n_row), col) for d in range(1, n_row)]
    by_col = [(row, lax.rem(col + d, n_col)) for d in range(1, n_col)]
    for peer in by_row + by_col:
        pl.semaphore_signal(barrier, inc=1, device_id=peer, device_id_type=MESH)
    for j in range(xs.shape[1]):
        xs[:, j, :] = x_ref[:, j * lanes : (j + 1) * lanes]
    pl.semaphore_wait(barrier, len(by_row) + len(by_col))
    started = []

    def send(src, dst, sems, d, peer):
        copy = pltpu.make_async_remote_copy(
            src_ref=src,
            dst_ref=dst,
            send_sem=sems[0].at[d],
            recv_sem=sems[1].at[d],
            device_id=peer,
            device_id_type=MESH,
        )
        copy.start()
        started.append(copy)
        return copy

    first = [
        send(xs.at[pl.ds(peer[1] * large, large)], land.at[d], (s1, r1), d, peer)
        for d, peer in enumerate(by_col)
    ]
    total = xs[pl.ds(col * large, large)]
    for d, copy in enumerate(first):
        copy.wait_recv()
        total = total + land[d]
    acc[...] = total
    second = [
        send(acc.at[pl.ds(peer[0] * small, small)], side.at[d], (s2, r2), d, peer)
        for d, peer in enumerate(by_row)
    ]
    total = acc[pl.ds(row * small, small)]
    for d, copy in enumerate(second):
        copy.wait_recv()
        total = total + side[d]
    mine = pl.ds(col * large + row * small, small)
    ys[mine] = total
    third = [send(ys.at[mine], ys.at[mine], (s3, r3), d, peer) for d, peer in enumerate(by_row)]
    for copy in third:
        copy.wait_recv()
    ours = pl.ds(col * large, large)
    fourth = [send(ys.at[ours], ys.at[ours], (s4, r4), d, peer) for d, peer in enumerate(by_col)]
    for copy in fourth:
        copy.wait_recv()
    for j in range(ys.shape[1]):
        o_ref[:, j * lanes : (j + 1) * lanes] = ys[:, j, :]
    for copy in started:
        copy.wait_send()


def reduce_all(x):
    n_row = lax.axis_size("row")
    n_col = lax.axis_size("col")
    rows, width = x.shape
    lanes = width // BLOCK
    large = rows // n_col
    small = large // n_row
    dma = pltpu.SemaphoreType.DMA
    row_sems = [dma((n_row - 1,))] * 2
    col_sems = [dma((n_col - 1,))] * 2
    return pl.pallas_call(
        functools.partial(reduce_kernel, n_row, n_col),
        out_shape=jax.ShapeDtypeStruct(x.shape, x.dtype),
        in_specs=[pl.BlockSpec(memory_space=pltpu.VMEM)],
        out_specs=pl.BlockSpec(memory_space=pltpu.VMEM),
        scratch_shapes=[
            pltpu.VMEM((rows, BLOCK, lanes), jnp.float32),
            pltpu.VMEM((rows, BLOCK, lanes), jnp.float32),
            pltpu.VMEM((n_col - 1, large, BLOCK, lanes), jnp.float32),
            pltpu.VMEM((large, BLOCK, lanes), jnp.float32),
            pltpu.VMEM((n_row - 1, small, BLOCK, lanes), jnp.float32),
        ]
        + col_sems
        + row_sems
        + row_sems
        + col_sems,
        compiler_params=pltpu.CompilerParams(
            collective_id=0, has_side_effects=True, vmem_limit_bytes=16 * 2**20
        ),
        cost_estimate=pl.CostEstimate(flops=10**6, bytes_accessed=6 * 10**7, transcendentals=0),
        name="reduce_all",
    )(x)


def split(x):
    high = x.astype(jnp.bfloat16)
    low = (x - high.astype(jnp.float32)).astype(jnp.bfloat16)
    return high, low


def join_kernel(
    sum_ref, count_ref, wpool_ref, att_ref, left_ref, right_ref, w_ref, up_ref, out_ref, branch, acc, moved
):
    step = pl.program_id(0) * 3 + pl.program_id(1)
    sheets, tall, cols, width = att_ref.shape
    place = lax.broadcasted_iota(jnp.int32, (cols, width), 0)

    def slide(side_ref, edge, by):
        for s in range(sheets):

            def one(r, carry):
                cells = pltpu.roll(att_ref[s, r].astype(jnp.float32), by, 0)
                side = side_ref[s, r].astype(jnp.float32)
                moved[s, r] = jnp.where(place == edge, side, cells).astype(jnp.bfloat16)
                return carry

            lax.fori_loop(0, tall, one, 0)

    @pl.when(step == 0)
    def _():
        slide(left_ref, 0, 1)

    @pl.when(step == 3)
    def _():
        moved[...] = att_ref[...]

    @pl.when(step == 6)
    def _():
        slide(right_ref, cols - 1, cols - 1)

    rows = out_ref.shape[1]
    ppm = wpool_ref.shape[2]
    total = sheets * BINS

    @pl.when(step == 0)
    def _():
        pooled = jnp.concatenate(split(sum_ref[...] / count_ref[...]), axis=0)
        slot = lax.broadcasted_iota(jnp.int32, (total, ppm), 0) % BINS
        start = 0
        for index, level in enumerate(pool_levels):
            here = (slot >= start) & (slot < start + level * level)
            start += level * level
            both = jnp.dot(pooled, wpool_ref[index], preferred_element_type=jnp.float32)
            grown = jnp.where(here, jnp.maximum(both[:total] + both[total:], 0.0), 0.0)
            high, low = split(grown)
            if level == 1:
                low = jnp.zeros_like(low)
            branch[:total, index * ppm : (index + 1) * ppm] = high
            branch[total:, index * ppm : (index + 1) * ppm] = low

    shift = pl.program_id(1)
    both = jnp.dot(branch[...], w_ref[0, 0, width:], preferred_element_type=jnp.float32)
    high, low = split(both[:total] + both[total:])
    for s in range(sheets):
        part = slice(s * BINS, (s + 1) * BINS)
        bins = jnp.concatenate([high[part], high[part], low[part]], axis=0)
        cells = moved[s, pl.ds(shift, rows)].reshape(rows * cols, width)
        term = jnp.dot(cells, w_ref[0, 0, :width], preferred_element_type=jnp.float32)
        term = term + jnp.dot(up_ref[0], bins, preferred_element_type=jnp.float32)

        @pl.when(step == 0)
        def _():
            acc[s] = term

        @pl.when(step != 0)
        def _():
            acc[s] = acc[s] + term

        @pl.when(step == 8)
        def _():
            out_ref[s] = acc[s].astype(jnp.bfloat16).reshape(rows, cols, -1)


def join(sums, counts, w_pool, tall, left, right, w_join, ups):
    sheets, rows2, cols, width = tall.shape
    rows = rows2 - 2
    cat, outs = w_join.shape[2:]
    ppm = w_pool.shape[2]
    return pl.pallas_call(
        join_kernel,
        grid=(3, 3),
        in_specs=[
            pl.BlockSpec(sums.shape, lambda c, a: (0, 0)),
            pl.BlockSpec(counts.shape, lambda c, a: (0, 0)),
            pl.BlockSpec(w_pool.shape, lambda c, a: (0, 0, 0)),
            pl.BlockSpec(tall.shape, lambda c, a: (0, 0, 0, 0)),
            pl.BlockSpec(left.shape, lambda c, a: (0, 0, 0, 0)),
            pl.BlockSpec(right.shape, lambda c, a: (0, 0, 0, 0)),
            pl.BlockSpec((1, 1, cat, outs), lambda c, a: (a, c, 0, 0)),
            pl.BlockSpec((1,) + ups.shape[1:], lambda c, a: (a * 3 + c, 0, 0)),
        ],
        out_specs=pl.BlockSpec((sheets, rows, cols, outs), lambda c, a: (0, 0, 0, 0)),
        out_shape=jax.ShapeDtypeStruct((sheets, rows, cols, outs), jnp.bfloat16),
        scratch_shapes=[
            pltpu.VMEM((2 * sheets * BINS, 4 * ppm), jnp.bfloat16),
            pltpu.VMEM((sheets, rows * cols, outs), jnp.float32),
            pltpu.VMEM(tall.shape, jnp.bfloat16),
        ],
        compiler_params=pltpu.CompilerParams(vmem_limit_bytes=48 * 2**20),
        name="join",
    )(sums, counts, w_pool, tall, left, right, w_join, ups)


def body(tokens, norm_gain, w_query, w_kv, w_out, w_pool, w_join):
    sheets, rows_here, cols_here, width = tokens.shape
    row_index = lax.axis_index("row")
    col_index = lax.axis_index("col")
    grid_h = rows_here * lax.axis_size("row")
    grid_w = cols_here * lax.axis_size("col")
    row_first = row_index * rows_here
    col_first = col_index * cols_here
    tokens_f = tokens.astype(jnp.float32)
    center = jnp.mean(tokens_f, axis=-1, keepdims=True)
    spread = jnp.mean((tokens_f - center) ** 2, axis=-1, keepdims=True)
    normed = ((tokens_f - center) * lax.rsqrt(spread + EPS) * norm_gain).astype(jnp.bfloat16)
    queries = jnp.dot(normed, w_query, preferred_element_type=jnp.float32)
    keyvals = jnp.dot(normed, w_kv, preferred_element_type=jnp.float32).astype(jnp.bfloat16)
    kv = padded(keyvals, (("row", 1), ("col", 2)), HALO).astype(jnp.float32)
    kv = jnp.pad(kv, ((0, 0), (0, 0), (0, WIDE - SPAN), (0, 0)))

    pools, counts, ups = [], [], []
    row_maps, col_maps = [], []
    for level in pool_levels:
        rows_in, rows_count = pool_matrix(level, grid_h, row_first, rows_here)
        cols_in, cols_count = pool_matrix(level, grid_w, col_first, cols_here)
        member = rows_in[:, None, :, None] & cols_in[None, :, None, :]
        pools.append(member.reshape(level * level, rows_here * cols_here))
        counts.append((rows_count[:, None] * cols_count[None, :]).reshape(-1))
        row_maps.append(upsample_matrix(level, grid_h, row_first - 1, rows_here + 2))
        col_maps.append(upsample_matrix(level, grid_w, col_first - 1, cols_here + 2))
    used = sum(level * level for level in pool_levels)
    pool = jnp.pad(jnp.concatenate(pools), ((0, BINS - used), (0, 0))).astype(jnp.bfloat16)
    bands = rows_here // BLOCK
    pool = pool.reshape(BINS, bands, BLOCK * cols_here).transpose(1, 0, 2)
    counts = jnp.pad(jnp.concatenate(counts), (0, BINS - used), constant_values=1)
    counts = jnp.tile(counts.astype(jnp.float32), sheets)[:, None]
    row_all = jnp.concatenate([jnp.repeat(m, l, axis=1) for m, l in zip(row_maps, pool_levels)], 1)
    col_all = jnp.concatenate([jnp.tile(m, (1, l)) for m, l in zip(col_maps, pool_levels)], 1)
    row_all = jnp.pad(row_all, ((0, 0), (0, BINS - used)))
    col_all = jnp.pad(col_all, ((0, 0), (0, BINS - used)))
    row_taps = jnp.stack([row_all[a : a + rows_here] for a in range(3)])
    col_taps = jnp.stack([col_all[c : c + cols_here] for c in range(3)])
    up = row_taps[:, None, :, None, :] * col_taps[None, :, None, :, :]
    up = up.reshape(9, rows_here * cols_here, BINS)
    up_high = lax.reduce_precision(up, 8, 7)
    up_low = (up - up_high).astype(jnp.bfloat16)
    up_high = up_high.astype(jnp.bfloat16)
    ups = jnp.concatenate([up_high, up_low, up_high], axis=-1)

    pos = jnp.stack([row_first, jnp.int32(grid_h), col_first, jnp.int32(grid_w)]).astype(jnp.int32)
    attended, partial = attend(pos, queries, kv, tokens, w_out, pool)
    sums = reduce_all(partial.reshape(sheets * BINS, width))
    tall = padded(attended, (("row", 1),), 1)
    n_col = lax.axis_size("col")
    ahead = [(i, (i + 1) % n_col) for i in range(n_col - 1)]
    back = [((i + 1) % n_col, i) for i in range(n_col - 1)]
    left = lax.ppermute(tall[:, :, cols_here - 1 :], "col", ahead)
    right = lax.ppermute(tall[:, :, :1], "col", back)
    return join(sums, counts, w_pool, tall, left, right, w_join, ups)


def solution(mesh):
    placed = (P(None, "row", "col", None), P(), P(), P(), P(), P(), P())
    return jax.shard_map(
        body, mesh=mesh, in_specs=placed, out_specs=P(None, "row", "col", None), check_vma=False
    )
```

```python
import functools
import math

import jax
import jax.numpy as jnp
from jax import lax
from jax.experimental import pallas as pl
from jax.experimental.pallas import tpu as pltpu
from jax.sharding import PartitionSpec as P

HEAD_DIM = 32
BLOCK = 8
HALO = 2
SPAN = BLOCK + 2 * HALO
WIDE = 16
LANES = 256
BINS = 64
MESH = pl.DeviceIdType.MESH

EPS = 1e-05
pool_levels = (1, 2, 3, 6)


def padded(cells, sides, width):
    for axis, dim in sides:
        count = lax.axis_size(axis)
        ends = count - 1
        head = lax.slice_in_dim(cells, 0, width, axis=dim)
        tail = lax.slice_in_dim(cells, cells.shape[dim] - width, cells.shape[dim], axis=dim)
        cells = jnp.concatenate(
            [
                lax.ppermute(tail, axis, [(i, (i + 1) % count) for i in range(ends)]),
                cells,
                lax.ppermute(head, axis, [((i + 1) % count, i) for i in range(ends)]),
            ],
            axis=dim,
        )
    return cells


def pool_matrix(level, length, first, count):
    places = first + jnp.arange(count)
    cells = jnp.arange(level)
    starts = cells * length // level
    ends = ((cells + 1) * length + level - 1) // level
    member = (places[None, :] >= starts[:, None]) & (places[None, :] < ends[:, None])
    return (member, ends - starts)


def upsample_matrix(level, length, first, count):
    places = first + jnp.arange(count)
    numer = jnp.maximum((2 * places + 1) * level - length, 0)
    lower = numer // (2 * length)
    frac = (numer - lower * 2 * length).astype(jnp.float32) / (2.0 * length)
    upper = jnp.minimum(lower + 1, level - 1)
    cells = jnp.arange(level)[None, :]
    weight = (cells == lower[:, None]) * (1.0 - frac)[:, None] + (cells == upper[:, None]) * frac[
        :, None
    ]
    inside = ((places >= 0) & (places < length)).astype(jnp.float32)
    return weight * inside[:, None]


def attend_kernel(pos, q_ref, kv_ref, tok_ref, wout_ref, pool_ref, att_ref, part_ref, ctx):
    band = pl.program_id(1)
    cols = q_ref.shape[2]
    inner = q_ref.shape[3]
    keys = SPAN * WIDE
    group = LANES // HEAD_DIM
    quers = BLOCK * BLOCK
    factor = math.log2(math.e) / math.sqrt(HEAD_DIM)
    place = lax.broadcasted_iota(jnp.int32, (keys, group * quers), 0)
    k_row = place // WIDE
    k_col = place % WIDE
    g_row = pos[0] + band * BLOCK - HALO + k_row
    row_ok = (g_row >= 0) & (g_row < pos[1]) & (k_col < SPAN)
    q_head = lax.broadcasted_iota(jnp.int32, (quers, LANES), 1) // HEAD_DIM
    rows = pl.ds(band * BLOCK, SPAN)
    for b in range(cols // BLOCK):
        g_col = pos[2] + b * BLOCK - HALO + k_col
        allowed = row_ok & (g_col >= 0) & (g_col < pos[3])
        for g in range(inner // LANES):
            lanes = slice(g * LANES, (g + 1) * LANES)
            vlanes = slice(inner + g * LANES, inner + (g + 1) * LANES)
            q = q_ref[0, :, b * BLOCK : (b + 1) * BLOCK, lanes].reshape(quers, LANES)
            wcols = slice(b * BLOCK, b * BLOCK + WIDE)
            k = kv_ref[0, rows, wcols, lanes].reshape(keys, LANES).astype(jnp.bfloat16)
            v = kv_ref[0, rows, wcols, vlanes].reshape(keys, LANES).astype(jnp.bfloat16)
            stack = jnp.concatenate(
                [jnp.where(q_head == h, q, 0.0) for h in range(group)], axis=0
            ).astype(jnp.bfloat16)
            scores = lax.dot_general(
                k, stack, (((1,), (1,)), ((), ())), preferred_element_type=jnp.float32
            )
            scores = jnp.where(allowed, scores, -1e30)
            top = jnp.max(scores, axis=0, keepdims=True)
            expon = jnp.exp2((scores - top) * factor)
            total = jnp.sum(expon, axis=0, keepdims=True)
            probs = (expon * (1.0 / total)).astype(jnp.bfloat16)
            out = lax.dot_general(
                v, probs, (((0,), (0,)), ((), ())), preferred_element_type=jnp.float32
            )
            pairs = jnp.concatenate(
                [
                    out[h * HEAD_DIM : (h + 1) * HEAD_DIM, (h // 2) * 2 * quers : (h // 2 + 1) * 2 * quers]
                    for h in range(group)
                ],
                axis=0,
            )
            turned = pairs.T
            got = jnp.where(q_head % 2 == 0, turned[:quers], turned[quers:])
            ctx[:, b * BLOCK : (b + 1) * BLOCK, lanes] = got.reshape(BLOCK, BLOCK, LANES)
    flat = ctx[...].reshape(BLOCK * cols, inner).astype(jnp.bfloat16)
    mixed = jnp.dot(flat, wout_ref[...], preferred_element_type=jnp.float32)
    tok = tok_ref[0].reshape(BLOCK * cols, -1).astype(jnp.float32)
    att = (tok + mixed).astype(jnp.bfloat16)
    att_ref[0] = att.reshape(BLOCK, cols, -1)
    part = jnp.dot(pool_ref[0], att, preferred_element_type=jnp.float32)

    @pl.when(band == 0)
    def _():
        part_ref[0] = part

    @pl.when(band != 0)
    def _():
        part_ref[0] = part_ref[0] + part


def attend(pos, queries, kv, tokens, w_out, pool):
    sheets, rows, cols, inner = queries.shape
    width = tokens.shape[-1]
    bands = rows // BLOCK
    return pl.pallas_call(
        attend_kernel,
        grid=(sheets, bands),
        in_specs=[
            pl.BlockSpec(memory_space=pltpu.SMEM),
            pl.BlockSpec((1, BLOCK, cols, inner), lambda s, a: (s, a, 0, 0)),
            pl.BlockSpec((1,) + kv.shape[1:], lambda s, a: (s, 0, 0, 0)),
            pl.BlockSpec((1, BLOCK, cols, width), lambda s, a: (s, a, 0, 0)),
            pl.BlockSpec(w_out.shape, lambda s, a: (0, 0)),
            pl.BlockSpec((1,) + pool.shape[1:], lambda s, a: (a, 0, 0)),
        ],
        out_specs=[
            pl.BlockSpec((1, BLOCK, cols, width), lambda s, a: (s, a, 0, 0)),
            pl.BlockSpec((1, BINS, width), lambda s, a: (s, 0, 0)),
        ],
        out_shape=[
            jax.ShapeDtypeStruct((sheets, rows, cols, width), jnp.bfloat16),
            jax.ShapeDtypeStruct((sheets, BINS, width), jnp.float32),
        ],
        scratch_shapes=[pltpu.VMEM((BLOCK, cols, inner), jnp.float32)],
        compiler_params=pltpu.CompilerParams(vmem_limit_bytes=40 * 2**20),
        name="attend",
    )(pos, queries, kv, tokens, w_out, pool)


def reduce_kernel(n_row, n_col, x_ref, o_ref, xs, ys, land, acc, side, s1, r1, s2, r2, s3, r3, s4, r4):
    row = lax.axis_index("row")
    col = lax.axis_index("col")
    large = acc.shape[0]
    small = side.shape[1]
    lanes = xs.shape[2]
    barrier = pltpu.get_barrier_semaphore()
    by_row = [(lax.rem(row + d, n_row), col) for d in range(1, n_row)]
    by_col = [(row, lax.rem(col + d, n_col)) for d in range(1, n_col)]
    for peer in by_row + by_col:
        pl.semaphore_signal(barrier, inc=1, device_id=peer, device_id_type=MESH)
    for j in range(xs.shape[1]):
        xs[:, j, :] = x_ref[:, j * lanes : (j + 1) * lanes]
    pl.semaphore_wait(barrier, len(by_row) + len(by_col))
    started = []

    def send(src, dst, sems, d, peer):
        copy = pltpu.make_async_remote_copy(
            src_ref=src,
            dst_ref=dst,
            send_sem=sems[0].at[d],
            recv_sem=sems[1].at[d],
            device_id=peer,
            device_id_type=MESH,
        )
        copy.start()
        started.append(copy)
        return copy

    first = [
        send(xs.at[pl.ds(peer[1] * large, large)], land.at[d], (s1, r1), d, peer)
        for d, peer in enumerate(by_col)
    ]
    total = xs[pl.ds(col * large, large)]
    for d, copy in enumerate(first):
        copy.wait_recv()
        total = total + land[d]
    acc[...] = total
    second = [
        send(acc.at[pl.ds(peer[0] * small, small)], side.at[d], (s2, r2), d, peer)
        for d, peer in enumerate(by_row)
    ]
    total = acc[pl.ds(row * small, small)]
    for d, copy in enumerate(second):
        copy.wait_recv()
        total = total + side[d]
    mine = pl.ds(col * large + row * small, small)
    ys[mine] = total
    third = [send(ys.at[mine], ys.at[mine], (s3, r3), d, peer) for d, peer in enumerate(by_row)]
    for copy in third:
        copy.wait_recv()
    ours = pl.ds(col * large, large)
    fourth = [send(ys.at[ours], ys.at[ours], (s4, r4), d, peer) for d, peer in enumerate(by_col)]
    for copy in fourth:
        copy.wait_recv()
    for j in range(ys.shape[1]):
        o_ref[:, j * lanes : (j + 1) * lanes] = ys[:, j, :]
    for copy in started:
        copy.wait_send()


def reduce_all(x):
    n_row = lax.axis_size("row")
    n_col = lax.axis_size("col")
    rows, width = x.shape
    lanes = width // BLOCK
    large = rows // n_col
    small = large // n_row
    dma = pltpu.SemaphoreType.DMA
    row_sems = [dma((n_row - 1,))] * 2
    col_sems = [dma((n_col - 1,))] * 2
    return pl.pallas_call(
        functools.partial(reduce_kernel, n_row, n_col),
        out_shape=jax.ShapeDtypeStruct(x.shape, x.dtype),
        in_specs=[pl.BlockSpec(memory_space=pltpu.VMEM)],
        out_specs=pl.BlockSpec(memory_space=pltpu.VMEM),
        scratch_shapes=[
            pltpu.VMEM((rows, BLOCK, lanes), jnp.float32),
            pltpu.VMEM((rows, BLOCK, lanes), jnp.float32),
            pltpu.VMEM((n_col - 1, large, BLOCK, lanes), jnp.float32),
            pltpu.VMEM((large, BLOCK, lanes), jnp.float32),
            pltpu.VMEM((n_row - 1, small, BLOCK, lanes), jnp.float32),
        ]
        + col_sems
        + row_sems
        + row_sems
        + col_sems,
        compiler_params=pltpu.CompilerParams(
            collective_id=0, has_side_effects=True, vmem_limit_bytes=16 * 2**20
        ),
        cost_estimate=pl.CostEstimate(flops=10**6, bytes_accessed=6 * 10**7, transcendentals=0),
        name="reduce_all",
    )(x)


def split(x):
    high = x.astype(jnp.bfloat16)
    low = (x - high.astype(jnp.float32)).astype(jnp.bfloat16)
    return high, low


def join_kernel(
    sum_ref, count_ref, wpool_ref, att_ref, left_ref, right_ref, w_ref, up_ref, out_ref, branch, acc, moved
):
    step = pl.program_id(0) * 3 + pl.program_id(1)
    sheets, tall, cols, width = att_ref.shape
    place = lax.broadcasted_iota(jnp.int32, (cols, width), 0)

    def slide(side_ref, edge, by):
        for s in range(sheets):

            def one(r, carry):
                cells = pltpu.roll(att_ref[s, r].astype(jnp.float32), by, 0)
                side = side_ref[s, r].astype(jnp.float32)
                moved[s, r] = jnp.where(place == edge, side, cells).astype(jnp.bfloat16)
                return carry

            lax.fori_loop(0, tall, one, 0)

    @pl.when(step == 0)
    def _():
        slide(left_ref, 0, 1)

    @pl.when(step == 3)
    def _():
        moved[...] = att_ref[...]

    @pl.when(step == 6)
    def _():
        slide(right_ref, cols - 1, cols - 1)

    rows = out_ref.shape[1]
    ppm = wpool_ref.shape[2]
    total = sheets * BINS

    @pl.when(step == 0)
    def _():
        pooled = jnp.concatenate(split(sum_ref[...] / count_ref[...]), axis=0)
        slot = lax.broadcasted_iota(jnp.int32, (total, ppm), 0) % BINS
        start = 0
        for index, level in enumerate(pool_levels):
            here = (slot >= start) & (slot < start + level * level)
            start += level * level
            both = jnp.dot(pooled, wpool_ref[index], preferred_element_type=jnp.float32)
            grown = jnp.where(here, jnp.maximum(both[:total] + both[total:], 0.0), 0.0)
            branch[:, index * ppm : (index + 1) * ppm] = grown.astype(jnp.bfloat16)

    shift = pl.program_id(1)
    both = jnp.dot(branch[...], w_ref[0, 0, width:], preferred_element_type=jnp.float32)
    high, low = split(both)
    for s in range(sheets):
        part = slice(s * BINS, (s + 1) * BINS)
        bins = jnp.concatenate([high[part], high[part], low[part]], axis=0)
        cells = moved[s, pl.ds(shift, rows)].reshape(rows * cols, width)
        term = jnp.dot(cells, w_ref[0, 0, :width], preferred_element_type=jnp.float32)
        term = term + jnp.dot(up_ref[0], bins, preferred_element_type=jnp.float32)

        @pl.when(step == 0)
        def _():
            acc[s] = term

        @pl.when(step != 0)
        def _():
            acc[s] = acc[s] + term

        @pl.when(step == 8)
        def _():
            out_ref[s] = acc[s].astype(jnp.bfloat16).reshape(rows, cols, -1)


def join(sums, counts, w_pool, tall, left, right, w_join, ups):
    sheets, rows2, cols, width = tall.shape
    rows = rows2 - 2
    cat, outs = w_join.shape[2:]
    ppm = w_pool.shape[2]
    return pl.pallas_call(
        join_kernel,
        grid=(3, 3),
        in_specs=[
            pl.BlockSpec(sums.shape, lambda c, a: (0, 0)),
            pl.BlockSpec(counts.shape, lambda c, a: (0, 0)),
            pl.BlockSpec(w_pool.shape, lambda c, a: (0, 0, 0)),
            pl.BlockSpec(tall.shape, lambda c, a: (0, 0, 0, 0)),
            pl.BlockSpec(left.shape, lambda c, a: (0, 0, 0, 0)),
            pl.BlockSpec(right.shape, lambda c, a: (0, 0, 0, 0)),
            pl.BlockSpec((1, 1, cat, outs), lambda c, a: (a, c, 0, 0)),
            pl.BlockSpec((1,) + ups.shape[1:], lambda c, a: (a * 3 + c, 0, 0)),
        ],
        out_specs=pl.BlockSpec((sheets, rows, cols, outs), lambda c, a: (0, 0, 0, 0)),
        out_shape=jax.ShapeDtypeStruct((sheets, rows, cols, outs), jnp.bfloat16),
        scratch_shapes=[
            pltpu.VMEM((sheets * BINS, 4 * ppm), jnp.bfloat16),
            pltpu.VMEM((sheets, rows * cols, outs), jnp.float32),
            pltpu.VMEM(tall.shape, jnp.bfloat16),
        ],
        compiler_params=pltpu.CompilerParams(vmem_limit_bytes=48 * 2**20),
        name="join",
    )(sums, counts, w_pool, tall, left, right, w_join, ups)


def body(tokens, norm_gain, w_query, w_kv, w_out, w_pool, w_join):
    sheets, rows_here, cols_here, width = tokens.shape
    row_index = lax.axis_index("row")
    col_index = lax.axis_index("col")
    grid_h = rows_here * lax.axis_size("row")
    grid_w = cols_here * lax.axis_size("col")
    row_first = row_index * rows_here
    col_first = col_index * cols_here
    tokens_f = tokens.astype(jnp.float32)
    center = jnp.mean(tokens_f, axis=-1, keepdims=True)
    spread = jnp.mean((tokens_f - center) ** 2, axis=-1, keepdims=True)
    normed = ((tokens_f - center) * lax.rsqrt(spread + EPS) * norm_gain).astype(jnp.bfloat16)
    queries = jnp.dot(normed, w_query, preferred_element_type=jnp.float32)
    keyvals = jnp.dot(normed, w_kv, preferred_element_type=jnp.float32).astype(jnp.bfloat16)
    kv = padded(keyvals, (("row", 1), ("col", 2)), HALO).astype(jnp.float32)
    kv = jnp.pad(kv, ((0, 0), (0, 0), (0, WIDE - SPAN), (0, 0)))

    pools, counts, ups = [], [], []
    row_maps, col_maps = [], []
    for level in pool_levels:
        rows_in, rows_count = pool_matrix(level, grid_h, row_first, rows_here)
        cols_in, cols_count = pool_matrix(level, grid_w, col_first, cols_here)
        member = rows_in[:, None, :, None] & cols_in[None, :, None, :]
        pools.append(member.reshape(level * level, rows_here * cols_here))
        counts.append((rows_count[:, None] * cols_count[None, :]).reshape(-1))
        row_maps.append(upsample_matrix(level, grid_h, row_first - 1, rows_here + 2))
        col_maps.append(upsample_matrix(level, grid_w, col_first - 1, cols_here + 2))
    used = sum(level * level for level in pool_levels)
    pool = jnp.pad(jnp.concatenate(pools), ((0, BINS - used), (0, 0))).astype(jnp.bfloat16)
    bands = rows_here // BLOCK
    pool = pool.reshape(BINS, bands, BLOCK * cols_here).transpose(1, 0, 2)
    counts = jnp.pad(jnp.concatenate(counts), (0, BINS - used), constant_values=1)
    counts = jnp.tile(counts.astype(jnp.float32), sheets)[:, None]
    row_all = jnp.concatenate([jnp.repeat(m, l, axis=1) for m, l in zip(row_maps, pool_levels)], 1)
    col_all = jnp.concatenate([jnp.tile(m, (1, l)) for m, l in zip(col_maps, pool_levels)], 1)
    row_all = jnp.pad(row_all, ((0, 0), (0, BINS - used)))
    col_all = jnp.pad(col_all, ((0, 0), (0, BINS - used)))
    row_taps = jnp.stack([row_all[a : a + rows_here] for a in range(3)])
    col_taps = jnp.stack([col_all[c : c + cols_here] for c in range(3)])
    up = row_taps[:, None, :, None, :] * col_taps[None, :, None, :, :]
    up = up.reshape(9, rows_here * cols_here, BINS)
    up_high = lax.reduce_precision(up, 8, 7)
    up_low = (up - up_high).astype(jnp.bfloat16)
    up_high = up_high.astype(jnp.bfloat16)
    ups = jnp.concatenate([up_high, up_low, up_high], axis=-1)

    pos = jnp.stack([row_first, jnp.int32(grid_h), col_first, jnp.int32(grid_w)]).astype(jnp.int32)
    attended, partial = attend(pos, queries, kv, tokens, w_out, pool)
    sums = reduce_all(partial.reshape(sheets * BINS, width))
    tall = padded(attended, (("row", 1),), 1)
    n_col = lax.axis_size("col")
    ahead = [(i, (i + 1) % n_col) for i in range(n_col - 1)]
    back = [((i + 1) % n_col, i) for i in range(n_col - 1)]
    left = lax.ppermute(tall[:, :, cols_here - 1 :], "col", ahead)
    right = lax.ppermute(tall[:, :, :1], "col", back)
    return join(sums, counts, w_pool, tall, left, right, w_join, ups)


def solution(mesh):
    placed = (P(None, "row", "col", None), P(), P(), P(), P(), P(), P())
    return jax.shard_map(
        body, mesh=mesh, in_specs=placed, out_specs=P(None, "row", "col", None), check_vma=False
    )
```
